32 devices in a mesh: lead: 4 (over x, core), space: 8 (over z, y).
Axes of the slice: x: 2, y: 2, z: 4, core: 2. Of those that a mesh axis runs over, the one named last changes fastest.
Arguments:
- states: bfloat16 [4, 4, 64, 128, 768], P('lead', None, 'space'), may hold values from -6 to 6
- filter_in: bfloat16 [2, 8, 96, 96], replicated, may hold values from -0.4375 to 0.4375
- filter_out: bfloat16 [2, 8, 96, 96], replicated, may hold values from -0.21875 to 0.21875
- filter_bias: float32 [2, 768], replicated, may hold values from -6 to 6
- decoder: bfloat16 [768, 128], replicated, may hold values from -0.5 to 0.5
- obs_value: float32 [4, 4, 32768], P('lead', None, 'space'), may hold values from -6 to 6
- obs_weight: float32 [4, 32768], P('lead', 'space'), may hold values from 0.5 to 2
- obs_index: int32 [4, 32768], P('lead', 'space'), may hold values from 0 to 131071
- block_dest: int32 [4, 256], P('lead', 'space'), may hold values from 0 to 7, as said below
- block_count: int32 [4, 256], P('lead', 'space'), may hold values from 96 to 128
Outputs:
- adjoint_fields: bfloat16 [4, 4, 64, 128, 768], P('lead', None, 'space')
The draws below stay inside these ranges and needn't reach their ends.
Inputs may be any that keep to these rules, and one draw needn't show every extreme that they name: `block_dest`: at most 8 blocks of one owner in one section name the same tile, and in each section one tile is named by exactly 8 blocks of every owner.
All inputs are finite; a program needn't handle non-finite values.
Results may differ from the reference program's by a relative error of at most 0.017.
Values may be sent and summed in bfloat16 or wider, within the bound.
A program may use at most 192 MiB of HBM per device.

```python
import math
import jax
import jax.numpy as jnp
from jax import lax

NLAT = 64
NLON = 128
C = 768
BS = 96
NVAR = 128
OBS_BLK = 128
BLK_DEV = 32
MEMBERS = 4
CAP = 8
SECTIONS = 4
NB = 8
CELLS_DEV = 1024
OBS_ROWS = 32768
N_SPACE = 8


def draw_block_dest(key, part):
    tiles = N_SPACE
    crowded = jax.random.randint(jax.random.fold_in(key, 11), (SECTIONS, 1, 1), 0, tiles)
    offset = jax.random.randint(jax.random.fold_in(key, 12), (SECTIONS, tiles, 1), 0, tiles - 1)
    position = jnp.arange(BLK_DEV, dtype=jnp.int32)[None, None, :]
    others = position - CAP
    spread = (crowded + 1 + (offset + others) % (tiles - 1)) % tiles
    target = jnp.where(position < CAP, crowded, spread)
    scores = jax.random.randint(jax.random.fold_in(key, 13), (SECTIONS, tiles, BLK_DEV), 0, 1 << 20) * BLK_DEV + position
    shuffle = jnp.argsort(scores, axis=2)
    target = jnp.take_along_axis(target, shuffle, axis=2)
    return target.reshape(SECTIONS, tiles * BLK_DEV).astype(jnp.int32)


def plant(array, stream_key, low, largest):
    extent = array.shape
    spot = [jax.random.randint(jax.random.fold_in(stream_key, axis), (), 0, extent[axis]) for axis in range(len(extent))]
    array = array.at[tuple(spot)].set(low)
    longest = extent.index(max(extent))
    spot[longest] = (spot[longest] + 1) % extent[longest]
    return array.at[tuple(spot)].set(largest)


def block_scale(stream_key, extent, shards, least, top_value):
    gain = 1.0
    for dim, parts in shards:
        heights = jax.random.uniform(jax.random.fold_in(jax.random.fold_in(stream_key, 6), dim), (parts,), jnp.float32, least / len(shards), top_value / len(shards))
        gain = gain * jnp.repeat(jnp.exp(heights), extent[dim] // parts).reshape((-1,) + (1,) * (len(extent) - 1 - dim))
    return gain


def gaussian(stream_key, extent, scale, most, pieces=(), kind=jnp.bfloat16):
    result = scale * jax.random.normal(stream_key, extent, jnp.float32)
    if pieces:
        result = result * block_scale(stream_key, extent, pieces, -0.22, 0.18)
    return jnp.clip(result, -most, most).astype(kind)


def setup_inputs(seed: int = 0) -> dict:
    streams_of = jax.random.split(jax.random.key(seed), 11)
    states = gaussian(streams_of[0], (SECTIONS, MEMBERS, NLAT, NLON, C), 1.0, 6.0, ((0, 4), (2, 8)))
    filter_in = gaussian(streams_of[1], (2, NB, BS, BS), (2 * BS) ** -0.5, 0.4375)
    filter_out = gaussian(streams_of[2], (2, NB, BS, BS), (8 * BS) ** -0.5, 0.21875)
    filter_bias = gaussian(streams_of[3], (2, C), 1.0, 6.0, (), jnp.float32)
    decoder = gaussian(streams_of[4], (C, NVAR), NVAR ** -0.5, 0.5)
    obs_value = gaussian(streams_of[5], (SECTIONS, MEMBERS, OBS_ROWS), 1.0, 6.0, ((0, 4), (2, 8)), jnp.float32)
    obs_weight = jnp.clip(jnp.exp(math.log(2.0) - 1.3862944 * jax.random.uniform(streams_of[6], (SECTIONS, OBS_ROWS), jnp.float32) ** block_scale(streams_of[6], (SECTIONS, OBS_ROWS), ((0, 4), (1, 8)), -0.2, 0.2)), 0.5, 2.0)
    obs_index = plant(jax.random.randint(streams_of[7], (SECTIONS, OBS_ROWS), 0, CELLS_DEV * NVAR), jax.random.fold_in(streams_of[7], 1), 0, (CELLS_DEV * NVAR) - 1).astype(jnp.int32)
    block_dest = draw_block_dest(jax.random.fold_in(streams_of[10], 71), 0)
    block_count = plant(jax.random.randint(streams_of[9], (SECTIONS, N_SPACE * BLK_DEV), 3 * OBS_BLK // 4, OBS_BLK + 1), jax.random.fold_in(streams_of[9], 1), 3 * OBS_BLK // 4, OBS_BLK).astype(jnp.int32)
    return {"states": states, "filter_in": filter_in, "filter_out": filter_out, "filter_bias": filter_bias, "decoder": decoder, "obs_value": obs_value, "obs_weight": obs_weight, "obs_index": obs_index, "block_dest": block_dest, "block_count": block_count}


root_scale = math.sqrt(2.0 / math.pi)
cubic_term = 0.044715

def gelu_slope(values):
    argument = root_scale * (values + cubic_term * values * values * values)
    tangent = jnp.tanh(argument)
    return 0.5 * (1.0 + tangent) + 0.5 * values * (1.0 - tangent * tangent) * root_scale * (1.0 + 3.0 * cubic_term * values * values)

def wave_table(row_count, col_count, length):
    row_index = lax.broadcasted_iota(jnp.int32, (row_count, col_count), 0)
    col_index = lax.broadcasted_iota(jnp.int32, (row_count, col_count), 1)
    angles = (row_index * col_index % length).astype(jnp.float32) * (2.0 * math.pi / length)
    return (jnp.cos(angles), jnp.sin(angles))

def make_tables(lon_len, lat_len):
    mode_count = lon_len // 2
    lon_scale = 1.0 / math.sqrt(lon_len)
    lat_scale = 1.0 / math.sqrt(lat_len)
    cos_fore, sin_fore = wave_table(lon_len, mode_count, lon_len)
    cos_back, sin_back = wave_table(mode_count, lon_len, lon_len)
    factor = jnp.where(lax.broadcasted_iota(jnp.int32, (mode_count, 1), 0) == 0, 1.0, 2.0).astype(jnp.float32)
    cos_lat, sin_lat = wave_table(lat_len, lat_len, lat_len)
    lon_cos = (cos_fore * lon_scale).astype(jnp.bfloat16)
    lon_sin = (-sin_fore * lon_scale).astype(jnp.bfloat16)
    back_cos = (factor * cos_back * lon_scale).astype(jnp.bfloat16)
    back_sin = (-factor * sin_back * lon_scale).astype(jnp.bfloat16)
    lat_cos = (cos_lat * lat_scale).astype(jnp.bfloat16)
    lat_sin = (sin_lat * lat_scale).astype(jnp.bfloat16)
    return (lon_cos, lon_sin, back_cos, back_sin, lat_cos, lat_sin)

def contract(pattern, left_op, right_op):
    return jnp.einsum(pattern, left_op.astype(jnp.float32), right_op.astype(jnp.float32), precision=lax.Precision.HIGHEST)

def block_mix(operand, matrix):
    split_view = operand.reshape(operand.shape[:-1] + (matrix.shape[0], matrix.shape[1]))
    return contract('...ni,nio->...no', split_view, matrix).reshape(operand.shape)

def block_mix_t(operand, matrix):
    split_view = operand.reshape(operand.shape[:-1] + (matrix.shape[0], matrix.shape[2]))
    return contract('...no,nio->...ni', split_view, matrix).reshape(operand.shape)

def section_modes(fields, tables, filter_in, filter_bias):
    lon_cos, lon_sin, lat_cos, lat_sin = (tables[0], tables[1], tables[4], tables[5])
    spec_re = contract('mfnc,nk->mfkc', fields, lon_cos).astype(jnp.bfloat16)
    spec_im = contract('mfnc,nk->mfkc', fields, lon_sin).astype(jnp.bfloat16)
    mode_re = (contract('pf,mfkc->mpkc', lat_cos, spec_re) + contract('pf,mfkc->mpkc', lat_sin, spec_im)).astype(jnp.bfloat16)
    mode_im = (contract('pf,mfkc->mpkc', lat_cos, spec_im) - contract('pf,mfkc->mpkc', lat_sin, spec_re)).astype(jnp.bfloat16)
    pre_re = block_mix(mode_re, filter_in[0]) - block_mix(mode_im, filter_in[1]) + filter_bias[0]
    pre_im = block_mix(mode_re, filter_in[1]) + block_mix(mode_im, filter_in[0]) + filter_bias[1]
    return (pre_re, pre_im)

def section_adjoint(incoming, pre_re, pre_im, tables, filter_in, filter_out):
    lon_cos, lon_sin, back_cos, back_sin, lat_cos, lat_sin = tables
    back_re = contract('mfnc,kn->mfkc', incoming, back_cos).astype(jnp.bfloat16)
    back_im = contract('mfnc,kn->mfkc', incoming, back_sin).astype(jnp.bfloat16)
    out_re = (contract('fp,mfkc->mpkc', lat_cos, back_re) + contract('fp,mfkc->mpkc', lat_sin, back_im)).astype(jnp.bfloat16)
    out_im = (contract('fp,mfkc->mpkc', lat_cos, back_im) - contract('fp,mfkc->mpkc', lat_sin, back_re)).astype(jnp.bfloat16)
    hid_re = block_mix_t(out_re, filter_out[0]) + block_mix_t(out_im, filter_out[1])
    hid_im = block_mix_t(out_im, filter_out[0]) - block_mix_t(out_re, filter_out[1])
    act_re = (hid_re * gelu_slope(pre_re)).astype(jnp.bfloat16)
    act_im = (hid_im * gelu_slope(pre_im)).astype(jnp.bfloat16)
    grad_re = (block_mix_t(act_re, filter_in[0]) + block_mix_t(act_im, filter_in[1])).astype(jnp.bfloat16)
    grad_im = (block_mix_t(act_im, filter_in[0]) - block_mix_t(act_re, filter_in[1])).astype(jnp.bfloat16)
    lat_re = (contract('pf,mpkc->mfkc', lat_cos, grad_re) - contract('pf,mpkc->mfkc', lat_sin, grad_im)).astype(jnp.bfloat16)
    lat_im = (contract('pf,mpkc->mfkc', lat_sin, grad_re) + contract('pf,mpkc->mfkc', lat_cos, grad_im)).astype(jnp.bfloat16)
    return contract('mfkc,nk->mfnc', lat_re, lon_cos) + contract('mfkc,nk->mfnc', lat_im, lon_sin)

def section_forcing(fields, decoder, values, weights, obs_cells, targets, counts):
    member_count, lat_len, lon_len = (fields.shape[0], fields.shape[1], fields.shape[2])
    levels = decoder.shape[1]
    decoded = contract('mfnc,cv->mfnv', fields, decoder).reshape(member_count, lat_len * lon_len * levels)
    row_total = obs_cells.shape[0]
    block_len = row_total // targets.shape[0]
    row_dest = jnp.repeat(targets, block_len, total_repeat_length=row_total)
    row_count = jnp.repeat(counts, block_len, total_repeat_length=row_total)
    within = jnp.arange(row_total, dtype=jnp.int32) % block_len
    weight_live = jnp.where(within < row_count, weights, 0.0)
    position = row_dest * (CELLS_DEV * levels) + obs_cells
    innovation = weight_live[None, :] * (decoded[:, position] - values)
    spread_sum = jnp.zeros_like(decoded).at[:, position].add(innovation).astype(jnp.bfloat16)
    return contract('mfnv,cv->mfnc', spread_sum.reshape(member_count, lat_len, lon_len, levels), decoder)

def reference(states, filter_in, filter_out, filter_bias, decoder, obs_value, obs_weight, obs_index, block_dest, block_count):
    tables = make_tables(states.shape[3], states.shape[2])
    incoming = jnp.zeros(states.shape[1:], jnp.bfloat16)
    results = []
    for section in range(SECTIONS - 1, -1, -1):
        fields = states[section]
        pre_re, pre_im = section_modes(fields, tables, filter_in, filter_bias)
        forcing = section_forcing(fields, decoder, obs_value[section], obs_weight[section], obs_index[section], block_dest[section], block_count[section])
        lift = section_adjoint(incoming, pre_re, pre_im, tables, filter_in, filter_out)
        incoming = (incoming.astype(jnp.float32) + lift + forcing).astype(jnp.bfloat16)
        results.append(incoming)
    return jnp.stack(results[::-1], 0)
```

```python
import math

import jax
import jax.numpy as jnp
from jax import lax
from jax.experimental import pallas as pl
from jax.experimental.pallas import tpu as pltpu
from jax.sharding import PartitionSpec as P

OBS_BLK = 128


root_scale = math.sqrt(2.0 / math.pi)
cubic_term = 0.044715


def gelu_slope(values):
    argument = root_scale * (values + cubic_term * values * values * values)
    tangent = jnp.tanh(argument)
    return 0.5 * (1.0 + tangent) + 0.5 * values * (1.0 - tangent * tangent) * root_scale * (
        1.0 + 3.0 * cubic_term * values * values
    )


def wave_table(row_count, col_count, length):
    row_index = lax.broadcasted_iota(jnp.int32, (row_count, col_count), 0)
    col_index = lax.broadcasted_iota(jnp.int32, (row_count, col_count), 1)
    angles = (row_index * col_index % length).astype(jnp.float32) * (2.0 * math.pi / length)
    return (jnp.cos(angles), jnp.sin(angles))


def make_tables(lon_len, lat_len):
    mode_count = lon_len // 2
    lon_scale = 1.0 / math.sqrt(lon_len)
    lat_scale = 1.0 / math.sqrt(lat_len)
    cos_fore, sin_fore = wave_table(lon_len, mode_count, lon_len)
    cos_back, sin_back = wave_table(mode_count, lon_len, lon_len)
    factor = jnp.where(lax.broadcasted_iota(jnp.int32, (mode_count, 1), 0) == 0, 1.0, 2.0).astype(
        jnp.float32
    )
    cos_lat, sin_lat = wave_table(lat_len, lat_len, lat_len)
    lon_cos = (cos_fore * lon_scale).astype(jnp.bfloat16)
    lon_sin = (-sin_fore * lon_scale).astype(jnp.bfloat16)
    back_cos = (factor * cos_back * lon_scale).astype(jnp.bfloat16)
    back_sin = (-factor * sin_back * lon_scale).astype(jnp.bfloat16)
    lat_cos = (cos_lat * lat_scale).astype(jnp.bfloat16)
    lat_sin = (sin_lat * lat_scale).astype(jnp.bfloat16)
    return (lon_cos, lon_sin, back_cos, back_sin, lat_cos, lat_sin)


def contract(pattern, left_op, right_op):
    return jnp.einsum(pattern, left_op, right_op, preferred_element_type=jnp.float32)


def block_mix(operand, matrix):
    split_view = operand.reshape(operand.shape[:-1] + (matrix.shape[0], matrix.shape[1]))
    return contract("...ni,nio->...no", split_view, matrix).reshape(operand.shape)


def block_mix_t(operand, matrix):
    split_view = operand.reshape(operand.shape[:-1] + (matrix.shape[0], matrix.shape[2]))
    return contract("...no,nio->...ni", split_view, matrix).reshape(operand.shape)


VMEM_BYTES = 56 * 1024 * 1024


def matmul(left, right):
    return jnp.dot(left, right, preferred_element_type=jnp.float32)


def rounded(values):
    return values.astype(jnp.bfloat16).astype(jnp.float32)


def turned(values):
    half = values.shape[1] // 2
    lanes = lax.broadcasted_iota(jnp.int32, values.shape, 1)
    rolled = pltpu.roll(values, half, 1)
    return jnp.where(lanes < half, rolled, -rolled)


def doubled(values):
    return jnp.concatenate([values, turned(values)], axis=0).astype(jnp.bfloat16)


def observe_kernel(cell_ref, level_ref, row_ref, high_ref, low_ref, out_ref, total):
    step = pl.program_id(0)

    @pl.when(step == 0)
    def _():
        total[...] = jnp.zeros_like(total)

    members, lats, levels, lons = out_ref.shape
    rows = cell_ref.shape[1]
    hot = (
        (lax.broadcasted_iota(jnp.int32, (lats * lons, rows), 0) == cell_ref[...])
        .astype(jnp.float32)
        .astype(jnp.bfloat16)
    )
    at_level = lax.broadcasted_iota(jnp.int32, (levels, rows), 0) == level_ref[...]
    picked = matmul(high_ref[...], hot) + matmul(low_ref[...], hot)
    weight = row_ref[0:1, :]
    spread = []
    for m in range(members):
        own = jnp.where(at_level, picked[m * levels : (m + 1) * levels], 0.0)
        innovation = weight * (jnp.sum(own, axis=0, keepdims=True) - row_ref[m + 1 : m + 2, :])
        spread.append(jnp.where(at_level, innovation, 0.0))
    spread = jnp.concatenate(spread, axis=0)
    high = spread.astype(jnp.bfloat16)
    low = (spread - high.astype(jnp.float32)).astype(jnp.bfloat16)
    dims = (((1,), (1,)), ((), ()))
    total[...] += lax.dot_general(
        high, hot, dims, preferred_element_type=jnp.float32
    ) + lax.dot_general(low, hot, dims, preferred_element_type=jnp.float32)

    @pl.when(step == pl.num_programs(0) - 1)
    def _():
        for m in range(members):
            for f in range(lats):
                out_ref[m, f] = total[
                    m * levels : (m + 1) * levels, f * lons : (f + 1) * lons
                ].astype(jnp.bfloat16)


def observe(received, fields, decoder):
    members, lats, lons, channels = fields.shape
    levels = decoder.shape[1]
    decoded = contract("mfnc,cv->mvfn", fields, decoder).reshape(members * levels, lats * lons)
    high = decoded.astype(jnp.bfloat16)
    low = (decoded - high.astype(jnp.float32)).astype(jnp.bfloat16)
    flat = jnp.swapaxes(received, 0, 1).reshape(members + 2, -1)
    count = flat.shape[1]
    index = flat[1:2].astype(jnp.int32)
    rows = jnp.concatenate([flat[:1], flat[2:]], axis=0)
    chunk = next(size for size in (512, 256, 128) if count % size == 0)
    whole = lambda i: (0, 0)
    piece = lambda i: (0, i)
    return pl.pallas_call(
        observe_kernel,
        grid=(count // chunk,),
        in_specs=[
            pl.BlockSpec((1, chunk), piece),
            pl.BlockSpec((1, chunk), piece),
            pl.BlockSpec((members + 1, chunk), piece),
            pl.BlockSpec(high.shape, whole),
            pl.BlockSpec(low.shape, whole),
        ],
        out_specs=pl.BlockSpec((members, lats, levels, lons), lambda i: (0, 0, 0, 0)),
        out_shape=jax.ShapeDtypeStruct((members, lats, levels, lons), jnp.bfloat16),
        scratch_shapes=[pltpu.VMEM((members * levels, lats * lons), jnp.float32)],
        compiler_params=pltpu.CompilerParams(vmem_limit_bytes=VMEM_BYTES),
        cost_estimate=pl.CostEstimate(
            flops=8 * count * members * levels * lats * lons,
            bytes_accessed=8 * members * levels * lats * lons,
            transcendentals=0,
        ),
        name="observe",
    )(index // levels, index % levels, rows, high, low)


def slope_kernel(spec_ref, lat_ref, mix_ref, bias_ref, out_ref, hold):
    lats, width, waves = spec_ref.shape

    @pl.loop(0, lats, unroll=4)
    def _(f):
        hold[pl.ds(pl.multiple_of(f * width, 8), width), :] = spec_ref[f].astype(jnp.float32)

    @pl.loop(0, width, unroll=8)
    def _(c):
        place = pl.ds(c, lats, stride=width)
        hold[place, :] = rounded(matmul(lat_ref[...], doubled(hold[place, :])))

    @pl.loop(0, lats, unroll=4)
    def _(p):
        modes = hold[pl.ds(pl.multiple_of(p * width, 8), width), :]
        before = matmul(mix_ref[...], doubled(modes)) + bias_ref[...]
        out_ref[p] = gelu_slope(before).astype(jnp.bfloat16)


def slopes(spec, lat_fore, mix, bias):
    lats, width, waves = spec.shape
    return pl.pallas_call(
        slope_kernel,
        out_shape=jax.ShapeDtypeStruct(spec.shape, jnp.bfloat16),
        scratch_shapes=[pltpu.VMEM((lats * width, waves), jnp.float32)],
        compiler_params=pltpu.CompilerParams(vmem_limit_bytes=VMEM_BYTES),
        cost_estimate=pl.CostEstimate(
            flops=4 * lats * width * waves * (lats + width),
            bytes_accessed=4 * lats * width * waves,
            transcendentals=lats * width * waves,
        ),
        name="slopes",
    )(spec, lat_fore, mix, bias)


def adjoint_kernel(
    in_ref,
    gain_ref,
    level_ref,
    decoder_ref,
    outer_ref,
    inner_ref,
    back_ref,
    fore_ref,
    ret_ref,
    lift_ref,
    out_ref,
    hold,
    force,
):
    width, lats, lons = in_ref.shape

    @pl.loop(0, lats, unroll=8)
    def _(f):
        force[pl.ds(f, width, stride=lats), :] = matmul(decoder_ref[...], level_ref[f])

    @pl.loop(0, width, unroll=8)
    def _(c):
        back = rounded(matmul(in_ref[c], back_ref[...]))
        hold[pl.ds(c, lats, stride=width), :] = rounded(matmul(fore_ref[...], doubled(back)))

    @pl.loop(0, lats, unroll=8)
    def _(p):
        place = pl.ds(pl.multiple_of(p * width, 8), width)
        hidden = matmul(outer_ref[...], doubled(hold[place, :]))
        act = rounded(hidden * gain_ref[p].astype(jnp.float32))
        hold[place, :] = rounded(matmul(inner_ref[...], doubled(act)))

    @pl.loop(0, width, unroll=8)
    def _(c):
        grad = doubled(hold[pl.ds(c, lats, stride=width), :])
        waves = matmul(ret_ref[...], grad).astype(jnp.bfloat16)
        added = matmul(waves, lift_ref[...]) + force[pl.ds(pl.multiple_of(c * lats, 8), lats), :]
        out_ref[c] = (in_ref[c].astype(jnp.float32) + added).astype(jnp.bfloat16)


def adjoint_step(incoming, gain, level_forcing, *weights):
    width, lats, lons = incoming.shape
    waves = gain.shape[2]
    return pl.pallas_call(
        adjoint_kernel,
        out_shape=jax.ShapeDtypeStruct(incoming.shape, jnp.bfloat16),
        scratch_shapes=[
            pltpu.VMEM((lats * width, waves), jnp.float32),
            pltpu.VMEM((lats * width, lons), jnp.float32),
        ],
        compiler_params=pltpu.CompilerParams(vmem_limit_bytes=VMEM_BYTES),
        cost_estimate=pl.CostEstimate(
            flops=8 * lats * width * waves * (lats + width + lons),
            bytes_accessed=10 * lats * width * waves,
            transcendentals=0,
        ),
        name="adjoint",
    )(incoming, gain, level_forcing, *weights)


def channel_plan(fields, filter_in, filter_out, filter_bias, decoder, received):
    member_count, lat_local, lon_len, channels = fields.shape
    tiles = lax.axis_size("space")
    sections = lax.axis_size("lead")
    me = lax.axis_index("space")
    width = filter_in.shape[2]
    lon_cos, lon_sin, back_cos, back_sin, lat_cos, lat_sin = make_tables(lon_len, lat_local * tiles)
    lon_fore = jnp.concatenate([lon_cos, lon_sin], axis=1)
    lon_back = jnp.concatenate([back_cos, back_sin], axis=0).T
    lat_fore = jnp.concatenate([lat_cos, lat_sin], axis=1)
    lat_back = jnp.concatenate([lat_cos.T, lat_sin.T], axis=1)
    lat_ret = jnp.concatenate([lat_cos.T, -lat_sin.T], axis=1)
    first = lax.dynamic_index_in_dim(filter_in, me, 1, keepdims=False)
    second = lax.dynamic_index_in_dim(filter_out, me, 1, keepdims=False)
    mix = jnp.concatenate([first[0].T, -first[1].T], axis=1)
    outer = jnp.concatenate([second[0], second[1]], axis=1)
    inner = jnp.concatenate([first[0], first[1]], axis=1)
    bias_own = lax.dynamic_slice_in_dim(filter_bias, me * width, width, 1)
    bias = jnp.repeat(bias_own.T, lon_len // 2, axis=1, total_repeat_length=lon_len)
    decoder_own = lax.dynamic_slice_in_dim(decoder, me * width, width, 0)

    gains = []
    for m in range(member_count):
        spec = contract("fnc,nk->fck", fields[m], lon_fore).astype(jnp.bfloat16)
        spec = lax.all_to_all(spec, "space", split_axis=1, concat_axis=0, tiled=True)
        gains.append(slopes(spec, lat_fore, mix, bias))
    forcing = observe(received, fields, decoder)
    forcing = lax.all_to_all(forcing, "lead", split_axis=0, concat_axis=0, tiled=True)
    forcing = lax.all_gather(forcing, "space", axis=1, tiled=True)
    gain = lax.all_to_all(jnp.stack(gains), "lead", split_axis=0, concat_axis=0, tiled=True)

    incoming = jnp.zeros((width, lat_local * tiles, lon_len), jnp.bfloat16)
    results = []
    for section in range(sections - 1, -1, -1):
        incoming = adjoint_step(
            incoming,
            gain[section],
            forcing[section],
            decoder_own,
            outer,
            inner,
            lon_back,
            lat_back,
            lat_ret,
            lon_fore.T,
        )
        results.append(lax.all_to_all(incoming, "space", split_axis=1, concat_axis=0, tiled=True))
    grouped = jnp.stack(results[::-1], 0)
    moved = lax.all_to_all(grouped, "lead", split_axis=0, concat_axis=0, tiled=True)
    return jnp.transpose(moved, (0, 2, 3, 1))[None]


def shards(
    states,
    filter_in,
    filter_out,
    filter_bias,
    decoder,
    obs_value,
    obs_weight,
    obs_index,
    block_dest,
    block_count,
):
    fields = states[0]
    member_count, lat_local, lon_len, channels = fields.shape
    tiles = lax.axis_size("space")
    block_total = block_dest.shape[1]
    slot_cap = 2 * ((block_total + tiles - 1) // tiles)
    live_rows = lax.broadcasted_iota(jnp.int32, (block_total, OBS_BLK), 1) < block_count[0][:, None]
    weight_rows = jnp.where(live_rows, obs_weight[0].reshape(block_total, OBS_BLK), 0.0)
    index_rows = obs_index[0].reshape(block_total, OBS_BLK).astype(jnp.float32)
    value_rows = jnp.swapaxes(obs_value[0].reshape(member_count, block_total, OBS_BLK), 0, 1)
    payload = jnp.concatenate([weight_rows[:, None], index_rows[:, None], value_rows], axis=1)
    targets = block_dest[0]
    matches = (targets[:, None] == lax.broadcasted_iota(jnp.int32, (block_total, tiles), 1)).astype(
        jnp.int32
    )
    earlier = jnp.cumsum(matches, axis=0) - matches
    slot_rank = jnp.sum(earlier * matches, axis=1)
    positions = targets * slot_cap + slot_rank
    outbox = (
        jnp.zeros((tiles * slot_cap, member_count + 2, OBS_BLK), jnp.float32)
        .at[positions]
        .set(payload)
    )
    received = lax.all_to_all(outbox, "space", split_axis=0, concat_axis=0, tiled=True)
    share_one = member_count == lax.axis_size("lead")
    aligned = lon_len % 128 == 0 and decoder.shape[1] % 128 == 0 and filter_in.shape[2] % 16 == 0
    if filter_in.shape[1] == tiles and share_one and aligned:
        return channel_plan(fields, filter_in, filter_out, filter_bias, decoder, received)
    lon_cos, lon_sin, back_cos, back_sin, lat_cos, lat_sin = make_tables(lon_len, lat_local * tiles)
    spec_re = contract("mfnc,nk->mfkc", fields, lon_cos).astype(jnp.bfloat16)
    spec_im = contract("mfnc,nk->mfkc", fields, lon_sin).astype(jnp.bfloat16)
    piece_re = lax.all_to_all(spec_re, "space", split_axis=2, concat_axis=1, tiled=True)
    piece_im = lax.all_to_all(spec_im, "space", split_axis=2, concat_axis=1, tiled=True)
    mode_re = (
        contract("pf,mfkc->mpkc", lat_cos, piece_re) + contract("pf,mfkc->mpkc", lat_sin, piece_im)
    ).astype(jnp.bfloat16)
    mode_im = (
        contract("pf,mfkc->mpkc", lat_cos, piece_im) - contract("pf,mfkc->mpkc", lat_sin, piece_re)
    ).astype(jnp.bfloat16)
    pre_re = block_mix(mode_re, filter_in[0]) - block_mix(mode_im, filter_in[1]) + filter_bias[0]
    pre_im = block_mix(mode_re, filter_in[1]) + block_mix(mode_im, filter_in[0]) + filter_bias[1]
    slope_re = gelu_slope(pre_re)
    slope_im = gelu_slope(pre_im)
    got_weight = received[:, 0].reshape(-1)
    got_index = received[:, 1].reshape(-1).astype(jnp.int32)
    got_value = jnp.swapaxes(received[:, 2:], 0, 1).reshape(member_count, -1)
    levels = decoder.shape[1]
    decoded = contract("mfnc,cv->mfnv", fields, decoder).reshape(member_count, -1)
    innovation = got_weight[None, :] * (decoded[:, got_index] - got_value)
    spread_sum = jnp.zeros_like(decoded).at[:, got_index].add(innovation).astype(jnp.bfloat16)
    forcing = contract(
        "mfnv,cv->mfnc", spread_sum.reshape(member_count, lat_local, lon_len, levels), decoder
    )

    def adjoint_layer(incoming, gain_re, gain_im):
        back_re = contract("mfnc,kn->mfkc", incoming, back_cos).astype(jnp.bfloat16)
        back_im = contract("mfnc,kn->mfkc", incoming, back_sin).astype(jnp.bfloat16)
        wave_re, wave_im = (
            lax.all_to_all(back_re, "space", split_axis=2, concat_axis=1, tiled=True),
            lax.all_to_all(back_im, "space", split_axis=2, concat_axis=1, tiled=True),
        )
        out_re = (
            contract("fp,mfkc->mpkc", lat_cos, wave_re)
            + contract("fp,mfkc->mpkc", lat_sin, wave_im)
        ).astype(jnp.bfloat16)
        out_im = (
            contract("fp,mfkc->mpkc", lat_cos, wave_im)
            - contract("fp,mfkc->mpkc", lat_sin, wave_re)
        ).astype(jnp.bfloat16)
        hid_re = block_mix_t(out_re, filter_out[0]) + block_mix_t(out_im, filter_out[1])
        hid_im = block_mix_t(out_im, filter_out[0]) - block_mix_t(out_re, filter_out[1])
        act_re = (hid_re * gain_re).astype(jnp.bfloat16)
        act_im = (hid_im * gain_im).astype(jnp.bfloat16)
        grad_re = (block_mix_t(act_re, filter_in[0]) + block_mix_t(act_im, filter_in[1])).astype(
            jnp.bfloat16
        )
        grad_im = (block_mix_t(act_im, filter_in[0]) - block_mix_t(act_re, filter_in[1])).astype(
            jnp.bfloat16
        )
        lat_re = (
            contract("pf,mpkc->mfkc", lat_cos, grad_re)
            - contract("pf,mpkc->mfkc", lat_sin, grad_im)
        ).astype(jnp.bfloat16)
        lat_im = (
            contract("pf,mpkc->mfkc", lat_sin, grad_re)
            + contract("pf,mpkc->mfkc", lat_cos, grad_im)
        ).astype(jnp.bfloat16)
        ret_re, ret_im = (
            lax.all_to_all(lat_re, "space", split_axis=1, concat_axis=2, tiled=True),
            lax.all_to_all(lat_im, "space", split_axis=1, concat_axis=2, tiled=True),
        )
        return contract("mfkc,nk->mfnc", ret_re, lon_cos) + contract(
            "mfkc,nk->mfnc", ret_im, lon_sin
        )

    lead_count = lax.axis_size("lead")
    moved_forcing, moved_re, moved_im = (
        lax.all_to_all(
            forcing[None].astype(jnp.bfloat16), "lead", split_axis=1, concat_axis=0, tiled=True
        ).astype(jnp.float32),
        lax.all_to_all(
            slope_re[None].astype(jnp.bfloat16), "lead", split_axis=1, concat_axis=0, tiled=True
        ).astype(jnp.float32),
        lax.all_to_all(
            slope_im[None].astype(jnp.bfloat16), "lead", split_axis=1, concat_axis=0, tiled=True
        ).astype(jnp.float32),
    )
    share = member_count // lead_count

    def local_turn(counter, state_pair):
        incoming, result = state_pair
        section = lead_count - 1 - counter
        sec_re = lax.dynamic_index_in_dim(moved_re, section, 0, keepdims=False)
        sec_im = lax.dynamic_index_in_dim(moved_im, section, 0, keepdims=False)
        sec_forcing = lax.dynamic_index_in_dim(moved_forcing, section, 0, keepdims=False)
        updated = (
            incoming.astype(jnp.float32) + adjoint_layer(incoming, sec_re, sec_im) + sec_forcing
        ).astype(jnp.bfloat16)
        return (updated, lax.dynamic_update_index_in_dim(result, updated, section, 0))

    start_field = jnp.zeros((share,) + fields.shape[1:], jnp.bfloat16)
    start_result = jnp.zeros((lead_count, share) + fields.shape[1:], jnp.bfloat16)
    grouped = lax.fori_loop(0, lead_count, local_turn, (start_field, start_result))[1]
    return lax.all_to_all(grouped, "lead", split_axis=0, concat_axis=1, tiled=True)


def solution(mesh):
    placed = (
        P("lead", None, "space", None, None),
        P(),
        P(),
        P(),
        P(),
        P("lead", None, "space"),
        P("lead", "space"),
        P("lead", "space"),
        P("lead", "space"),
        P("lead", "space"),
    )
    return jax.shard_map(
        shards,
        mesh=mesh,
        in_specs=placed,
        out_specs=P("lead", None, "space", None, None),
        check_vma=False,
    )
```

```python
import math

import jax
import jax.numpy as jnp
import numpy as np
from jax import lax
from jax.experimental import pallas as pl
from jax.experimental.pallas import tpu as pltpu
from jax.sharding import PartitionSpec as P

OBS_BLK = 128


root_scale = math.sqrt(2.0 / math.pi)
cubic_term = 0.044715


def gelu_slope(values):
    argument = root_scale * (values + cubic_term * values * values * values)
    tangent = jnp.tanh(argument)
    return 0.5 * (1.0 + tangent) + 0.5 * values * (1.0 - tangent * tangent) * root_scale * (
        1.0 + 3.0 * cubic_term * values * values
    )


def wave_table(row_count, col_count, length):
    row_index = lax.broadcasted_iota(jnp.int32, (row_count, col_count), 0)
    col_index = lax.broadcasted_iota(jnp.int32, (row_count, col_count), 1)
    angles = (row_index * col_index % length).astype(jnp.float32) * (2.0 * math.pi / length)
    return (jnp.cos(angles), jnp.sin(angles))


def make_tables(lon_len, lat_len):
    mode_count = lon_len // 2
    lon_scale = 1.0 / math.sqrt(lon_len)
    lat_scale = 1.0 / math.sqrt(lat_len)
    cos_fore, sin_fore = wave_table(lon_len, mode_count, lon_len)
    cos_back, sin_back = wave_table(mode_count, lon_len, lon_len)
    factor = jnp.where(lax.broadcasted_iota(jnp.int32, (mode_count, 1), 0) == 0, 1.0, 2.0).astype(
        jnp.float32
    )
    cos_lat, sin_lat = wave_table(lat_len, lat_len, lat_len)
    lon_cos = (cos_fore * lon_scale).astype(jnp.bfloat16)
    lon_sin = (-sin_fore * lon_scale).astype(jnp.bfloat16)
    back_cos = (factor * cos_back * lon_scale).astype(jnp.bfloat16)
    back_sin = (-factor * sin_back * lon_scale).astype(jnp.bfloat16)
    lat_cos = (cos_lat * lat_scale).astype(jnp.bfloat16)
    lat_sin = (sin_lat * lat_scale).astype(jnp.bfloat16)
    return (lon_cos, lon_sin, back_cos, back_sin, lat_cos, lat_sin)


def fixed_tables(lon_len, lat_len):
    def waves(rows, cols, length):
        angles = (np.arange(rows)[:, None] * np.arange(cols)[None, :] % length).astype(np.float32)
        angles = angles * np.float32(2.0 * math.pi / length)
        return np.cos(angles), np.sin(angles)

    modes = lon_len // 2
    lon_scale = np.float32(1.0 / math.sqrt(lon_len))
    lat_scale = np.float32(1.0 / math.sqrt(lat_len))
    cos, sin = waves(lon_len, modes, lon_len)
    lon = np.concatenate([cos, -sin], axis=1) * lon_scale
    factor = np.where(np.arange(2 * modes) % modes == 0, 1.0, 2.0).astype(np.float32)
    lat_cos, lat_sin = (part * lat_scale for part in waves(lat_len, lat_len, lat_len))
    found = (
        lon,
        lon * factor,
        np.concatenate([lat_cos, lat_sin], axis=1),
        np.concatenate([lat_cos.T, lat_sin.T], axis=1),
        np.concatenate([lat_cos.T, -lat_sin.T], axis=1),
        lon.T,
    )
    return tuple(jnp.asarray(table.astype(jnp.bfloat16)) for table in found)


def contract(pattern, left_op, right_op):
    return jnp.einsum(pattern, left_op, right_op, preferred_element_type=jnp.float32)


def block_mix(operand, matrix):
    split_view = operand.reshape(operand.shape[:-1] + (matrix.shape[0], matrix.shape[1]))
    return contract("...ni,nio->...no", split_view, matrix).reshape(operand.shape)


def block_mix_t(operand, matrix):
    split_view = operand.reshape(operand.shape[:-1] + (matrix.shape[0], matrix.shape[2]))
    return contract("...no,nio->...ni", split_view, matrix).reshape(operand.shape)


VMEM_BYTES = 56 * 1024 * 1024


def matmul(left, right):
    return jnp.dot(left, right, preferred_element_type=jnp.float32)


def rounded(values):
    return values.astype(jnp.bfloat16).astype(jnp.float32)


def turned(values):
    half = values.shape[1] // 2
    lanes = lax.broadcasted_iota(jnp.int32, values.shape, 1)
    rolled = pltpu.roll(values, half, 1)
    return jnp.where(lanes < half, rolled, -rolled)


def tied(value, *others):
    return lax.optimization_barrier((value,) + others)[0]


def doubled(values):
    return jnp.concatenate([values, turned(values)], axis=0).astype(jnp.bfloat16)


def observe_kernel(cell_ref, level_ref, row_ref, high_ref, low_ref, out_ref, total):
    step = pl.program_id(0)

    @pl.when(step == 0)
    def _():
        total[...] = jnp.zeros_like(total)

    members, lats, levels, lons = out_ref.shape
    rows = cell_ref.shape[1]
    hot = (
        (lax.broadcasted_iota(jnp.int32, (lats * lons, rows), 0) == cell_ref[...])
        .astype(jnp.float32)
        .astype(jnp.bfloat16)
    )
    at_level = lax.broadcasted_iota(jnp.int32, (levels, rows), 0) == level_ref[...]
    picked = matmul(high_ref[...], hot) + matmul(low_ref[...], hot)
    weight = row_ref[0:1, :]
    spread = []
    for m in range(members):
        own = jnp.where(at_level, picked[m * levels : (m + 1) * levels], 0.0)
        innovation = weight * (jnp.sum(own, axis=0, keepdims=True) - row_ref[m + 1 : m + 2, :])
        spread.append(jnp.where(at_level, innovation, 0.0))
    spread = jnp.concatenate(spread, axis=0)
    high = spread.astype(jnp.bfloat16)
    low = (spread - high.astype(jnp.float32)).astype(jnp.bfloat16)
    dims = (((1,), (1,)), ((), ()))
    total[...] += lax.dot_general(
        high, hot, dims, preferred_element_type=jnp.float32
    ) + lax.dot_general(low, hot, dims, preferred_element_type=jnp.float32)

    @pl.when(step == pl.num_programs(0) - 1)
    def _():
        for m in range(members):
            for f in range(lats):
                out_ref[m, f] = total[
                    m * levels : (m + 1) * levels, f * lons : (f + 1) * lons
                ].astype(jnp.bfloat16)


def observe(received, fields, decoder):
    members, lats, lons, channels = fields.shape
    levels = decoder.shape[1]
    decoded = contract("mfnc,cv->mvfn", fields, decoder).reshape(members * levels, lats * lons)
    high = decoded.astype(jnp.bfloat16)
    low = (decoded - high.astype(jnp.float32)).astype(jnp.bfloat16)
    flat = jnp.swapaxes(received, 0, 1).reshape(members + 2, -1)
    count = flat.shape[1]
    index = flat[1:2].astype(jnp.int32)
    rows = jnp.concatenate([flat[:1], flat[2:]], axis=0)
    chunk = next(size for size in (512, 256, 128) if count % size == 0)
    whole = lambda i: (0, 0)
    piece = lambda i: (0, i)
    return pl.pallas_call(
        observe_kernel,
        grid=(count // chunk,),
        in_specs=[
            pl.BlockSpec((1, chunk), piece),
            pl.BlockSpec((1, chunk), piece),
            pl.BlockSpec((members + 1, chunk), piece),
            pl.BlockSpec(high.shape, whole),
            pl.BlockSpec(low.shape, whole),
        ],
        out_specs=pl.BlockSpec((members, lats, levels, lons), lambda i: (0, 0, 0, 0)),
        out_shape=jax.ShapeDtypeStruct((members, lats, levels, lons), jnp.bfloat16),
        scratch_shapes=[pltpu.VMEM((members * levels, lats * lons), jnp.float32)],
        compiler_params=pltpu.CompilerParams(vmem_limit_bytes=VMEM_BYTES),
        cost_estimate=pl.CostEstimate(
            flops=8 * count * members * levels * lats * lons,
            bytes_accessed=8 * members * levels * lats * lons,
            transcendentals=0,
        ),
        name="observe",
    )(index // levels, index % levels, rows, high, low)


def spectrum_kernel(which_ref, state_ref, table_ref, *rest):
    out_ref = rest[-1]
    parts, _, width, waves = out_ref.shape
    dims = (((0,), (0,)), ((), ()))
    spec = lax.dot_general(
        state_ref[0, 0], table_ref[...], dims, preferred_element_type=jnp.float32
    )
    out_ref[:, 0] = spec.reshape(parts, width, waves).astype(jnp.bfloat16)


def spectrum_of(fields, which, table, parts, *before):
    members, lats, lons, channels = fields.shape
    width = channels // parts
    waves = table.shape[1]
    spec = pltpu.PrefetchScalarGridSpec(
        num_scalar_prefetch=1,
        grid=(lats,),
        in_specs=[
            pl.BlockSpec((1, 1, lons, channels), lambda f, which_ref: (which_ref[0], f, 0, 0)),
            pl.BlockSpec((lons, waves), lambda f, which_ref: (0, 0)),
        ]
        + [pl.BlockSpec(memory_space=pl.ANY)] * len(before),
        out_specs=pl.BlockSpec((parts, 1, width, waves), lambda f, which_ref: (0, f, 0, 0)),
    )
    return pl.pallas_call(
        spectrum_kernel,
        grid_spec=spec,
        out_shape=jax.ShapeDtypeStruct((parts, lats, width, waves), jnp.bfloat16),
        compiler_params=pltpu.CompilerParams(vmem_limit_bytes=VMEM_BYTES),
        cost_estimate=pl.CostEstimate(
            flops=2 * lats * lons * channels * waves,
            bytes_accessed=4 * lats * lons * channels,
            transcendentals=0,
        ),
        name="spectrum",
    )(which.reshape(1), fields, table, *before)


def slope_kernel(spec_ref, lat_ref, mix_ref, bias_ref, out_ref, hold):
    lats, width, waves = spec_ref.shape

    @pl.loop(0, lats, unroll=4)
    def _(f):
        hold[pl.ds(pl.multiple_of(f * width, 8), width), :] = spec_ref[f].astype(jnp.float32)

    @pl.loop(0, width, unroll=8)
    def _(c):
        place = pl.ds(c, lats, stride=width)
        hold[place, :] = rounded(matmul(lat_ref[...], doubled(hold[place, :])))

    @pl.loop(0, lats, unroll=4)
    def _(p):
        modes = hold[pl.ds(pl.multiple_of(p * width, 8), width), :]
        before = matmul(mix_ref[...], doubled(modes)) + bias_ref[...]
        out_ref[p] = gelu_slope(before).astype(jnp.bfloat16)


def slopes(spec, lat_fore, mix, bias):
    lats, width, waves = spec.shape
    return pl.pallas_call(
        slope_kernel,
        out_shape=jax.ShapeDtypeStruct(spec.shape, jnp.bfloat16),
        scratch_shapes=[pltpu.VMEM((lats * width, waves), jnp.float32)],
        compiler_params=pltpu.CompilerParams(vmem_limit_bytes=VMEM_BYTES),
        cost_estimate=pl.CostEstimate(
            flops=4 * lats * width * waves * (lats + width),
            bytes_accessed=4 * lats * width * waves,
            transcendentals=lats * width * waves,
        ),
        name="slopes",
    )(spec, lat_fore, mix, bias)


def adjoint_kernel(
    in_ref,
    gain_ref,
    level_ref,
    decoder_ref,
    outer_ref,
    inner_ref,
    back_ref,
    fore_ref,
    ret_ref,
    lift_ref,
    out_ref,
    hold,
    force,
):
    width, lats, lons = in_ref.shape

    @pl.loop(0, lats, unroll=8)
    def _(f):
        force[pl.ds(f, width, stride=lats), :] = matmul(decoder_ref[...], level_ref[f])

    @pl.loop(0, width, unroll=8)
    def _(c):
        back = rounded(matmul(in_ref[c], back_ref[...]))
        hold[pl.ds(c, lats, stride=width), :] = rounded(matmul(fore_ref[...], doubled(back)))

    @pl.loop(0, lats, unroll=8)
    def _(p):
        place = pl.ds(pl.multiple_of(p * width, 8), width)
        hidden = matmul(outer_ref[...], doubled(hold[place, :]))
        act = rounded(hidden * gain_ref[p].astype(jnp.float32))
        hold[place, :] = rounded(matmul(inner_ref[...], doubled(act)))

    @pl.loop(0, width, unroll=8)
    def _(c):
        grad = doubled(hold[pl.ds(c, lats, stride=width), :])
        waves = matmul(ret_ref[...], grad).astype(jnp.bfloat16)
        added = matmul(waves, lift_ref[...]) + force[pl.ds(pl.multiple_of(c * lats, 8), lats), :]
        out_ref[c] = (in_ref[c].astype(jnp.float32) + added).astype(jnp.bfloat16)


def adjoint_step(incoming, gain, level_forcing, *weights):
    width, lats, lons = incoming.shape
    waves = gain.shape[2]
    return pl.pallas_call(
        adjoint_kernel,
        out_shape=jax.ShapeDtypeStruct(incoming.shape, jnp.bfloat16),
        scratch_shapes=[
            pltpu.VMEM((lats * width, waves), jnp.float32),
            pltpu.VMEM((lats * width, lons), jnp.float32),
        ],
        compiler_params=pltpu.CompilerParams(vmem_limit_bytes=VMEM_BYTES),
        cost_estimate=pl.CostEstimate(
            flops=8 * lats * width * waves * (lats + width + lons),
            bytes_accessed=10 * lats * width * waves,
            transcendentals=0,
        ),
        name="adjoint",
    )(incoming, gain, level_forcing, *weights)


def channel_plan(fields, filter_in, filter_out, filter_bias, decoder, received):
    member_count, lat_local, lon_len, channels = fields.shape
    tiles = lax.axis_size("space")
    sections = lax.axis_size("lead")
    me = lax.axis_index("space")
    width = filter_in.shape[2]
    lon_fore, lon_back, lat_fore, lat_back, lat_ret, lon_lift = fixed_tables(
        lon_len, lat_local * tiles
    )
    first = lax.dynamic_index_in_dim(filter_in, me, 1, keepdims=False)
    second = lax.dynamic_index_in_dim(filter_out, me, 1, keepdims=False)
    mix = jnp.concatenate([first[0].T, -first[1].T], axis=1)
    outer = jnp.concatenate([second[0], second[1]], axis=1)
    inner = jnp.concatenate([first[0], first[1]], axis=1)
    bias_own = lax.dynamic_slice_in_dim(filter_bias, me * width, width, 1)
    bias = jnp.repeat(bias_own.T, lon_len // 2, axis=1, total_repeat_length=lon_len)
    decoder_own = lax.dynamic_slice_in_dim(decoder, me * width, width, 0)

    turns = [t for t in range(1, sections)] + [0]
    turns = turns[1:2] + turns[:1] + turns[2:]
    lead = lax.axis_index("lead")

    def own_index(turn):
        return lax.rem(lead + turn, sections)

    def hand_over(piece, turn):
        if turn == 0:
            return piece
        return lax.ppermute(piece, "lead", [(i, (i + turn) % sections) for i in range(sections)])

    def section_of(arrived, section):
        stacked = jnp.stack([arrived[t] for t in range(sections)])
        return lax.dynamic_index_in_dim(
            stacked, lax.rem(lead + sections - section, sections), 0, keepdims=False
        )

    gains = {}
    level_parts = {}
    made = []
    for order, turn in enumerate(turns):
        before = ()
        if order == 1:
            before = (forcing,)
        if order > 1:
            before = (made[order - 2],)
        spec = spectrum_of(fields, own_index(turn), lon_fore, tiles, *before)
        spec = lax.all_to_all(spec, "space", split_axis=0, concat_axis=0, tiled=True)
        spec = spec.reshape((-1,) + spec.shape[2:])
        if order == 0:
            forcing = observe(received, fields, decoder)
        if order == sections - 1:
            last_spec = spec
        made.append(slopes(spec, lat_fore, mix, bias))
        gains[turn] = hand_over(made[-1], turn)
    for turn in turns:
        piece = lax.dynamic_index_in_dim(forcing, own_index(turn), 0, keepdims=False)
        level_parts[turn] = hand_over(piece, turn)
    levels = [section_of(level_parts, section) for section in range(sections)]
    top = sections - 1
    top_level = lax.all_gather(tied(levels[top], last_spec), "space", axis=0, tiled=True)
    rest = lax.all_gather(
        tied(jnp.stack(levels[:top]), last_spec), "space", axis=1, tiled=True
    )

    incoming = jnp.zeros((width, lat_local * tiles, lon_len), jnp.bfloat16)
    results = {}
    for section in range(top, -1, -1):
        if section + 2 in results:
            incoming = tied(incoming, results[section + 2])
        incoming = adjoint_step(
            incoming,
            section_of(gains, section),
            top_level if section == top else rest[section],
            decoder_own,
            outer,
            inner,
            lon_back,
            lat_back,
            lat_ret,
            lon_lift,
        )
        results[section] = lax.all_to_all(
            incoming, "space", split_axis=1, concat_axis=0, tiled=True
        )
    grouped = jnp.stack([results[section] for section in range(sections)], 0)
    moved = lax.all_to_all(grouped, "lead", split_axis=0, concat_axis=0, tiled=True)
    return jnp.transpose(moved, (0, 2, 3, 1))[None]


def shards(
    states,
    filter_in,
    filter_out,
    filter_bias,
    decoder,
    obs_value,
    obs_weight,
    obs_index,
    block_dest,
    block_count,
):
    fields = states[0]
    member_count, lat_local, lon_len, channels = fields.shape
    tiles = lax.axis_size("space")
    block_total = block_dest.shape[1]
    slot_cap = 2 * ((block_total + tiles - 1) // tiles)
    live_rows = lax.broadcasted_iota(jnp.int32, (block_total, OBS_BLK), 1) < block_count[0][:, None]
    weight_rows = jnp.where(live_rows, obs_weight[0].reshape(block_total, OBS_BLK), 0.0)
    index_rows = obs_index[0].reshape(block_total, OBS_BLK).astype(jnp.float32)
    value_rows = jnp.swapaxes(obs_value[0].reshape(member_count, block_total, OBS_BLK), 0, 1)
    payload = jnp.concatenate([weight_rows[:, None], index_rows[:, None], value_rows], axis=1)
    targets = block_dest[0]
    matches = (targets[:, None] == lax.broadcasted_iota(jnp.int32, (block_total, tiles), 1)).astype(
        jnp.int32
    )
    earlier = jnp.cumsum(matches, axis=0) - matches
    slot_rank = jnp.sum(earlier * matches, axis=1)
    positions = targets * slot_cap + slot_rank
    outbox = (
        jnp.zeros((tiles * slot_cap, member_count + 2, OBS_BLK), jnp.float32)
        .at[positions]
        .set(payload)
    )
    received = lax.all_to_all(outbox, "space", split_axis=0, concat_axis=0, tiled=True)
    share_one = member_count == lax.axis_size("lead")
    aligned = lon_len % 128 == 0 and decoder.shape[1] % 128 == 0 and filter_in.shape[2] % 16 == 0
    if filter_in.shape[1] == tiles and share_one and aligned:
        return channel_plan(fields, filter_in, filter_out, filter_bias, decoder, received)
    lon_cos, lon_sin, back_cos, back_sin, lat_cos, lat_sin = make_tables(lon_len, lat_local * tiles)
    spec_re = contract("mfnc,nk->mfkc", fields, lon_cos).astype(jnp.bfloat16)
    spec_im = contract("mfnc,nk->mfkc", fields, lon_sin).astype(jnp.bfloat16)
    piece_re = lax.all_to_all(spec_re, "space", split_axis=2, concat_axis=1, tiled=True)
    piece_im = lax.all_to_all(spec_im, "space", split_axis=2, concat_axis=1, tiled=True)
    mode_re = (
        contract("pf,mfkc->mpkc", lat_cos, piece_re) + contract("pf,mfkc->mpkc", lat_sin, piece_im)
    ).astype(jnp.bfloat16)
    mode_im = (
        contract("pf,mfkc->mpkc", lat_cos, piece_im) - contract("pf,mfkc->mpkc", lat_sin, piece_re)
    ).astype(jnp.bfloat16)
    pre_re = block_mix(mode_re, filter_in[0]) - block_mix(mode_im, filter_in[1]) + filter_bias[0]
    pre_im = block_mix(mode_re, filter_in[1]) + block_mix(mode_im, filter_in[0]) + filter_bias[1]
    slope_re = gelu_slope(pre_re)
    slope_im = gelu_slope(pre_im)
    got_weight = received[:, 0].reshape(-1)
    got_index = received[:, 1].reshape(-1).astype(jnp.int32)
    got_value = jnp.swapaxes(received[:, 2:], 0, 1).reshape(member_count, -1)
    levels = decoder.shape[1]
    decoded = contract("mfnc,cv->mfnv", fields, decoder).reshape(member_count, -1)
    innovation = got_weight[None, :] * (decoded[:, got_index] - got_value)
    spread_sum = jnp.zeros_like(decoded).at[:, got_index].add(innovation).astype(jnp.bfloat16)
    forcing = contract(
        "mfnv,cv->mfnc", spread_sum.reshape(member_count, lat_local, lon_len, levels), decoder
    )

    def adjoint_layer(incoming, gain_re, gain_im):
        back_re = contract("mfnc,kn->mfkc", incoming, back_cos).astype(jnp.bfloat16)
        back_im = contract("mfnc,kn->mfkc", incoming, back_sin).astype(jnp.bfloat16)
        wave_re, wave_im = (
            lax.all_to_all(back_re, "space", split_axis=2, concat_axis=1, tiled=True),
            lax.all_to_all(back_im, "space", split_axis=2, concat_axis=1, tiled=True),
        )
        out_re = (
            contract("fp,mfkc->mpkc", lat_cos, wave_re)
            + contract("fp,mfkc->mpkc", lat_sin, wave_im)
        ).astype(jnp.bfloat16)
        out_im = (
            contract("fp,mfkc->mpkc", lat_cos, wave_im)
            - contract("fp,mfkc->mpkc", lat_sin, wave_re)
        ).astype(jnp.bfloat16)
        hid_re = block_mix_t(out_re, filter_out[0]) + block_mix_t(out_im, filter_out[1])
        hid_im = block_mix_t(out_im, filter_out[0]) - block_mix_t(out_re, filter_out[1])
        act_re = (hid_re * gain_re).astype(jnp.bfloat16)
        act_im = (hid_im * gain_im).astype(jnp.bfloat16)
        grad_re = (block_mix_t(act_re, filter_in[0]) + block_mix_t(act_im, filter_in[1])).astype(
            jnp.bfloat16
        )
        grad_im = (block_mix_t(act_im, filter_in[0]) - block_mix_t(act_re, filter_in[1])).astype(
            jnp.bfloat16
        )
        lat_re = (
            contract("pf,mpkc->mfkc", lat_cos, grad_re)
            - contract("pf,mpkc->mfkc", lat_sin, grad_im)
        ).astype(jnp.bfloat16)
        lat_im = (
            contract("pf,mpkc->mfkc", lat_sin, grad_re)
            + contract("pf,mpkc->mfkc", lat_cos, grad_im)
        ).astype(jnp.bfloat16)
        ret_re, ret_im = (
            lax.all_to_all(lat_re, "space", split_axis=1, concat_axis=2, tiled=True),
            lax.all_to_all(lat_im, "space", split_axis=1, concat_axis=2, tiled=True),
        )
        return contract("mfkc,nk->mfnc", ret_re, lon_cos) + contract(
            "mfkc,nk->mfnc", ret_im, lon_sin
        )

    lead_count = lax.axis_size("lead")
    moved_forcing, moved_re, moved_im = (
        lax.all_to_all(
            forcing[None].astype(jnp.bfloat16), "lead", split_axis=1, concat_axis=0, tiled=True
        ).astype(jnp.float32),
        lax.all_to_all(
            slope_re[None].astype(jnp.bfloat16), "lead", split_axis=1, concat_axis=0, tiled=True
        ).astype(jnp.float32),
        lax.all_to_all(
            slope_im[None].astype(jnp.bfloat16), "lead", split_axis=1, concat_axis=0, tiled=True
        ).astype(jnp.float32),
    )
    share = member_count // lead_count

    def local_turn(counter, state_pair):
        incoming, result = state_pair
        section = lead_count - 1 - counter
        sec_re = lax.dynamic_index_in_dim(moved_re, section, 0, keepdims=False)
        sec_im = lax.dynamic_index_in_dim(moved_im, section, 0, keepdims=False)
        sec_forcing = lax.dynamic_index_in_dim(moved_forcing, section, 0, keepdims=False)
        updated = (
            incoming.astype(jnp.float32) + adjoint_layer(incoming, sec_re, sec_im) + sec_forcing
        ).astype(jnp.bfloat16)
        return (updated, lax.dynamic_update_index_in_dim(result, updated, section, 0))

    start_field = jnp.zeros((share,) + fields.shape[1:], jnp.bfloat16)
    start_result = jnp.zeros((lead_count, share) + fields.shape[1:], jnp.bfloat16)
    grouped = lax.fori_loop(0, lead_count, local_turn, (start_field, start_result))[1]
    return lax.all_to_all(grouped, "lead", split_axis=0, concat_axis=1, tiled=True)


def solution(mesh):
    placed = (
        P("lead", None, "space", None, None),
        P(),
        P(),
        P(),
        P(),
        P("lead", None, "space"),
        P("lead", "space"),
        P("lead", "space"),
        P("lead", "space"),
        P("lead", "space"),
    )
    return jax.shard_map(
        shards,
        mesh=mesh,
        in_specs=placed,
        out_specs=P("lead", None, "space", None, None),
        check_vma=False,
    )
```
